1024 devices in a mesh: group: 32 (over x, y, core), local: 32 (over z).
Axes of the slice: x: 4, y: 4, z: 32, core: 2. Of those that a mesh axis runs over, the one named last changes fastest.
Arguments:
- tokens: bfloat16 [8192, 2048], P(('group', 'local')), may hold values from -6 to 6
- grad_mixed: bfloat16 [8192, 2048], P(('group', 'local')), may hold values from -6 to 6
- gates: bfloat16 [8192, 10], P(('group', 'local')), may hold values from 0.029907227 to 0.3984375
- group_ids: int32 [8192, 4], P(('group', 'local')), may hold values from 0 to 15, as said below
- expert_ids: int32 [8192, 10], P(('group', 'local')), may hold values from 0 to 511, as said below
- w_gate: bfloat16 [32, 32, 2048, 256], P('group', 'local'), may hold values from -0.125 to 0.125
- w_up: bfloat16 [32, 32, 2048, 256], P('group', 'local'), may hold values from -0.125 to 0.125
- w_down: bfloat16 [32, 32, 256, 2048], P('group', 'local'), may hold values from -0.25 to 0.25
Outputs:
- mixed: bfloat16 [8192, 2048], P(('group', 'local'))
- grad_tokens: bfloat16 [8192, 2048], P(('group', 'local'))
- grad_gates: float32 [8192, 10], P(('group', 'local'))
The draws below stay inside these ranges and needn't reach their ends.
Inputs may be any that keep to these rules, and one draw needn't show every extreme that they name: `group_ids`: each row names 4 different groups; the 8 rows of one device name every group exactly 2 times. `expert_ids`: row t names 10 different experts: three of group group_ids[t,0], three of group_ids[t,1], two of group_ids[t,2] and two of group_ids[t,3], in this order; expert G * 32 + j is number j of group G.
All inputs are finite; a program needn't handle non-finite values.
Results may differ from the reference program's by a relative error of at most 0.007.
Values may be sent and summed in bfloat16 or wider, within the bound.
No kernel may reach another device: no remote copies, remote signals or barrier semaphores. Data moves between devices by JAX's collectives and lax.ppermute only.
A program may use at most 32 MiB of HBM per device.

```python
import math
import jax
import jax.numpy as jnp
from jax import lax

D = 2048
FF = 512
TOK_DEV = 8
TOPK = 10
EXP_GRP = 32
EXPERTS = 512
FFH = 256
TOKENS = 8192
N_GROUP = 32
N_LOCAL = 32


def route_tables(key):
    devices = TOKENS // TOK_DEV
    groups_all = N_GROUP // 2
    orders = jax.vmap(lambda number: jax.random.permutation(jax.random.fold_in(key, number + 11), groups_all))(jnp.arange(devices, dtype=jnp.int32))
    cycle = (4 * jnp.arange(TOK_DEV, dtype=jnp.int32)[:, None] + jnp.arange(4, dtype=jnp.int32)[None, :]) % groups_all
    chosen = orders[:, cycle].reshape(TOKENS, 4).astype(jnp.int32)
    liking = jax.random.randint(jax.random.fold_in(key, 7), (groups_all, N_LOCAL), 0, 3)
    noise = jax.random.randint(jax.random.fold_in(key, 8), (TOKENS, 4, N_LOCAL), 0, 2 ** 19)
    scores = (liking[chosen] * 2 ** 18 + noise) * N_LOCAL + jnp.arange(N_LOCAL, dtype=jnp.int32)[None, None, :]
    best = lax.top_k(scores, 3)[1].astype(jnp.int32)
    experts = chosen[:, :, None] * N_LOCAL + best
    listed = jnp.concatenate([experts[:, 0, :3], experts[:, 1, :3], experts[:, 2, :2], experts[:, 3, :2]], axis=1)
    return (chosen, listed.astype(jnp.int32))


def draw_group_ids(key, part):
    return route_tables(key)[0]


def draw_expert_ids(key, part):
    return route_tables(key)[1]


def shard_levels(key, extent, cuts, least, largest):
    level, own = 1.0, jax.random.fold_in(key, 6)
    for dim, shards_of in cuts:
        heights = jnp.exp(jax.random.uniform(jax.random.fold_in(own, dim), (shards_of,), jnp.float32, least / len(cuts), largest / len(cuts)))
        level = level * jnp.repeat(heights, extent[dim] // shards_of).reshape([-1 if axis == dim else 1 for axis in range(len(extent))])
    return level


def bell_draw(rng, shape, spread, most, shards=(), kind=jnp.bfloat16):
    entries = spread * jax.random.normal(rng, shape, jnp.float32)
    if shards:
        entries = entries * shard_levels(rng, shape, shards, -0.22, 0.18)
    return jnp.clip(entries, -most, most).astype(kind)


def setup_inputs(seed: int = 0) -> dict:
    keys = jax.random.split(jax.random.key(seed), 9)
    tokens = bell_draw(keys[0], (TOKENS, D), 1.0, 6.0, ((0, 1024),))
    grad_mixed = bell_draw(keys[1], (TOKENS, D), 1.0, 6.0, ((0, 1024),))
    gates = jnp.clip(jnp.exp(math.log(0.3984375) - 2.5894505 * jax.random.uniform(keys[2], (TOKENS, TOPK), jnp.float32) ** shard_levels(keys[2], (TOKENS, TOPK), ((0, 1024),), -0.2, 0.2)), 0.029907227, 0.3984375).astype(jnp.bfloat16)
    group_ids = draw_group_ids(jax.random.fold_in(keys[8], 71), 0)
    expert_ids = draw_expert_ids(jax.random.fold_in(keys[8], 71), 0)
    w_gate = bell_draw(keys[5], (N_GROUP, EXP_GRP, D, FFH), D ** -0.5, 0.125, ((0, 32), (1, 32)))
    w_up = bell_draw(keys[6], (N_GROUP, EXP_GRP, D, FFH), D ** -0.5, 0.125, ((0, 32), (1, 32)))
    w_down = bell_draw(keys[7], (N_GROUP, EXP_GRP, FFH, D), FF ** -0.5, 0.25, ((0, 32), (1, 32)))
    return {"tokens": tokens, "grad_mixed": grad_mixed, "gates": gates, "group_ids": group_ids, "expert_ids": expert_ids, "w_gate": w_gate, "w_up": w_up, "w_down": w_down}


def expert_half(rows_x, rows_dy, rows_gate, w_in, w_lin, w_out):
    pre_gate = jnp.dot(rows_x, w_in, preferred_element_type=jnp.float32)
    pre_up = jnp.dot(rows_x, w_lin, preferred_element_type=jnp.float32)
    sigmoid = jax.nn.sigmoid(pre_gate)
    active = pre_gate * sigmoid
    hidden = (active * pre_up).astype(jnp.bfloat16)
    partial_out = jnp.dot(hidden, w_out, preferred_element_type=jnp.float32)
    scale = rows_gate.astype(jnp.float32)[:, None]
    weighted = (scale * partial_out).astype(jnp.bfloat16)
    gate_term = jnp.sum(rows_dy.astype(jnp.float32) * partial_out, axis=1).astype(jnp.bfloat16)
    scaled_dy = (scale * rows_dy.astype(jnp.float32)).astype(jnp.bfloat16)
    grad_hidden = lax.dot_general(scaled_dy, w_out, (((1,), (1,)), ((), ())), preferred_element_type=jnp.float32)
    grad_pre = (grad_hidden * pre_up * sigmoid * (1.0 + pre_gate * (1.0 - sigmoid))).astype(jnp.bfloat16)
    grad_lin = (grad_hidden * active).astype(jnp.bfloat16)
    back_rows = lax.dot_general(grad_pre, w_in, (((1,), (1,)), ((), ())), preferred_element_type=jnp.float32)
    back_rows = back_rows + lax.dot_general(grad_lin, w_lin, (((1,), (1,)), ((), ())), preferred_element_type=jnp.float32)
    return weighted, back_rows.astype(jnp.bfloat16), gate_term


def reference(tokens, grad_mixed, gates, group_ids, expert_ids, w_gate, w_up, w_down):
    capacity = (25 * TOK_DEV + N_LOCAL - 1) // N_LOCAL
    positions = jnp.arange(TOKENS, dtype=jnp.int32)
    local_of = (positions // TOK_DEV) % N_LOCAL
    named = jnp.any(group_ids[:, :, None] == (expert_ids // EXP_GRP)[:, None, :], axis=1)
    onehot = jnp.any((expert_ids[:, :, None] == jnp.arange(EXPERTS, dtype=jnp.int32)[None, None, :]) & named[:, :, None], axis=1).astype(jnp.int32)
    blocks = onehot.reshape(N_GROUP, N_LOCAL, TOK_DEV, EXPERTS).transpose(1, 0, 2, 3).reshape(N_LOCAL, N_GROUP * TOK_DEV, EXPERTS)
    before = jnp.cumsum(blocks, axis=1) - blocks
    before = before.reshape(N_LOCAL, N_GROUP, TOK_DEV, EXPERTS).transpose(1, 0, 2, 3).reshape(TOKENS, EXPERTS)
    ranking = jnp.take_along_axis(before, expert_ids, axis=1)
    kept = named & (ranking < capacity)
    slot_rank = jnp.where(kept, ranking, capacity).reshape(-1).astype(jnp.int32)
    flat_expert = expert_ids.reshape(-1)
    flat_local = jnp.repeat(local_of, TOPK)
    flat_token = jnp.repeat(positions, TOPK)
    flat_choice = jnp.tile(jnp.arange(TOPK, dtype=jnp.int32), TOKENS)
    token_table = jnp.full((EXPERTS, N_LOCAL, capacity), -1, jnp.int32).at[flat_expert, flat_local, slot_rank].set(flat_token, mode="drop")
    choice_table = jnp.zeros((EXPERTS, N_LOCAL, capacity), jnp.int32).at[flat_expert, flat_local, slot_rank].set(flat_choice, mode="drop")

    def per_expert(totals, expert):
        out_acc, back_acc, gate_acc = totals
        slot_rows = token_table[expert].reshape(-1)
        slot_choice = choice_table[expert].reshape(-1)
        is_valid = slot_rows >= 0
        safe_rows = jnp.maximum(slot_rows, 0)
        rows_x = jnp.where(is_valid[:, None], tokens[safe_rows], jnp.zeros((), jnp.bfloat16))
        rows_dy = jnp.where(is_valid[:, None], grad_mixed[safe_rows], jnp.zeros((), jnp.bfloat16))
        rows_gate = jnp.where(is_valid, gates[safe_rows, slot_choice], jnp.zeros((), jnp.bfloat16))
        group_of = expert // N_LOCAL
        member = expert % N_LOCAL
        for which_half in range(2):
            index_row = 2 * group_of + which_half
            weighted, back_rows, gate_term = expert_half(rows_x, rows_dy, rows_gate, w_gate[index_row, member], w_up[index_row, member], w_down[index_row, member])
            out_acc = out_acc.at[safe_rows].add(weighted.astype(jnp.float32))
            back_acc = back_acc.at[safe_rows].add(back_rows.astype(jnp.float32))
            gate_acc = gate_acc.at[safe_rows, slot_choice].add(gate_term.astype(jnp.float32))
        return (out_acc, back_acc, gate_acc), None

    start = (jnp.zeros((TOKENS, D), jnp.float32), jnp.zeros((TOKENS, D), jnp.float32), jnp.zeros((TOKENS, TOPK), jnp.float32))
    finals, unused = lax.scan(per_expert, start, jnp.arange(EXPERTS, dtype=jnp.int32))
    out_acc, back_acc, gate_acc = finals
    return out_acc.astype(jnp.bfloat16), back_acc.astype(jnp.bfloat16), gate_acc
```

```python
import jax
import jax.numpy as jnp
from jax import lax
from jax.sharding import PartitionSpec as P

BF = jnp.bfloat16
F32 = jnp.float32
META = 128


def dot(a, b, dims):
    return lax.dot_general(a, b, (dims, ((), ())), preferred_element_type=F32)


def body(tokens, grad_mixed, gates, group_ids, expert_ids, w_gate, w_up, w_down):
    n_group = lax.axis_size("group")
    n_local = lax.axis_size("local")
    near = 8 if n_local % 8 == 0 and n_local > 8 else n_local // 2
    far = n_local // near
    groups = n_group // 2
    tok = tokens.shape[0]
    width = tokens.shape[1]
    half = width // 2
    topk = expert_ids.shape[1]
    named = group_ids.shape[1]
    per_group = named * tok // groups
    capacity = (25 * tok + n_local - 1) // n_local
    pad = (capacity // 8 + 1) * 8
    me = lax.axis_index("group")
    my_group = (me // 2).astype(BF)
    core = me % 2
    z = lax.axis_index("local")

    def shift(array, by):
        return lax.ppermute(array, "local", [(i, (i + by) % n_local) for i in range(n_local)])

    def swap(array):
        return lax.ppermute(array, "group", [(i, i ^ 1) for i in range(n_group)])

    meta = jnp.concatenate(
        [(expert_ids // n_local).astype(BF), (expert_ids % n_local).astype(BF), gates, group_ids.astype(BF)], axis=1
    )
    meta = jnp.pad(meta, ((0, 0), (0, META - meta.shape[1])))
    own = jnp.concatenate([tokens, grad_mixed, meta], axis=1)
    rows = jnp.concatenate([own] + [shift(own, near * f) for f in range(1, far)], axis=0)

    names = rows[:, 2 * width + 3 * topk : 2 * width + 3 * topk + named].reshape(far, tok, named)
    member = jnp.any(names[..., None] == jnp.arange(groups, dtype=F32).astype(BF), axis=2).astype(jnp.int32)
    placed = jnp.cumsum(member, axis=1) - member
    chooser = (
        (member.transpose(2, 0, 1)[:, :, None, :] == 1)
        & (placed.transpose(2, 0, 1)[:, :, None, :] == jnp.arange(per_group, dtype=jnp.int32)[None, None, :, None])
    ).astype(BF)
    chooser = chooser[:, :, :, None, :] * jnp.eye(far, dtype=BF)[None, :, None, :, None]
    chooser = chooser.reshape(groups * far * per_group, far * tok)
    parts = []
    for c in range(2):
        piece = jnp.concatenate(
            [rows[:, c * half : (c + 1) * half], rows[:, width + c * half : width + (c + 1) * half], rows[:, 2 * width :]],
            axis=1,
        )
        parts.append(dot(chooser, piece, ((1,), (0,))).astype(BF).reshape(groups, 1, far * per_group, width + META))
    send = jnp.concatenate(parts, axis=1).reshape(n_group, far * per_group, width + META)
    got = lax.all_to_all(send, "group", split_axis=0, concat_axis=0, tiled=True)
    n_rows = n_group * far * per_group
    got = got.reshape(n_rows, width + META)

    shifts = [s - (near // 2 - 1) for s in range(near)]
    info = got[:, width:].T
    row_group, row_pos, row_gate = info[:topk], info[topk : 2 * topk], info[2 * topk : 3 * topk]
    target = ((z + jnp.arange(near, dtype=jnp.int32) - (near // 2 - 1)) % n_local).astype(BF)
    picked = (row_group == my_group)[:, None, :] & (row_pos[:, None, :] == target[None, :, None])
    counted = jnp.any(picked, axis=0)
    gate_at = jnp.sum(jnp.where(picked, row_gate.astype(F32)[:, None, :], 0.0), axis=0)
    index = jnp.arange(n_rows, dtype=jnp.int32)
    plane_of = (index // per_group) % far
    ahead = ((index[:, None] < index[None, :]) & (plane_of[:, None] == plane_of[None, :])).astype(BF)
    ranked = dot(counted.astype(BF), ahead, ((1,), (0,))).astype(jnp.int32)
    kept = counted & (ranked < capacity)
    slot = jnp.where(kept, ranked, -1)
    hit = (slot[:, None, None, :] == jnp.arange(pad, dtype=jnp.int32)[None, None, :, None]) & (
        plane_of[None, None, None, :] == jnp.arange(far, dtype=jnp.int32)[None, :, None, None]
    )
    n_slots = near * far * pad
    plain = hit.astype(BF).reshape(n_slots, n_rows)
    scaled = jnp.where(hit, gate_at[:, None, None, :], 0.0).astype(BF).reshape(n_slots, n_rows)
    slot_x = dot(plain, got[:, :half], ((1,), (0,))).astype(BF)
    slot_dy = dot(scaled, got[:, half:width], ((1,), (0,))).astype(BF)
    slots = jnp.concatenate([slot_x, slot_dy], axis=1).reshape(near, far * pad, width)
    mine = jnp.concatenate(
        [slots[i] if s == 0 else shift(slots[i], s) for i, s in enumerate(shifts)], axis=0
    )

    other = swap(mine)
    first = jnp.where(core == 0, mine, other)
    second = jnp.where(core == 0, other, mine)
    x = jnp.concatenate([first[:, :half], second[:, :half]], axis=1)
    dy = jnp.concatenate([first[:, half:], second[:, half:]], axis=1)

    w_in, w_lin, w_out = w_gate[0, 0], w_up[0, 0], w_down[0, 0]
    pre_gate = dot(x, w_in, ((1,), (0,)))
    pre_up = dot(x, w_lin, ((1,), (0,)))
    sigmoid = jax.nn.sigmoid(pre_gate)
    active = pre_gate * sigmoid
    hidden = (active * pre_up).astype(BF)
    out = dot(hidden, w_out, ((1,), (0,)))
    grad_hidden = dot(dy, w_out, ((1,), (1,)))
    grad_pre = (grad_hidden * pre_up * sigmoid * (1.0 + pre_gate * (1.0 - sigmoid))).astype(BF)
    grad_lin = (grad_hidden * active).astype(BF)
    back = dot(grad_pre, w_in, ((1,), (1,))) + dot(grad_lin, w_lin, ((1,), (1,)))

    keep_out = jnp.where(core == 0, out[:, :half], out[:, half:])
    keep_back = jnp.where(core == 0, back[:, :half], back[:, half:])
    give_out = jnp.where(core == 0, out[:, half:], out[:, :half])
    give_back = jnp.where(core == 0, back[:, half:], back[:, :half])
    gave = swap(jnp.concatenate([give_out.astype(BF), give_back.astype(BF)], axis=1))
    sum_out = keep_out + gave[:, :half].astype(F32)
    sum_back = keep_back + gave[:, half:].astype(F32)
    term = jnp.sum(mine[:, half:].astype(F32) * sum_out, axis=1)
    lane = jnp.arange(half, dtype=jnp.int32)
    place = jnp.arange(pad, dtype=jnp.int32)
    spare = jnp.sum(
        jnp.where(lane[None, None, :] == place[None, :, None], term.reshape(near * far, pad, 1), 0.0), axis=1, keepdims=True
    )
    sum_out = jnp.where(
        (place == pad - 1)[None, :, None], spare, sum_out.reshape(near * far, pad, half)
    ).reshape(n_slots, half)
    ret = jnp.concatenate([sum_out.astype(BF), sum_back.astype(BF)], axis=1).reshape(near, far * pad, width)
    ret = jnp.concatenate(
        [ret[i] if s == 0 else shift(ret[i], -s) for i, s in enumerate(shifts)], axis=0
    )

    row_out = dot(scaled, ret[:, :half], ((0,), (0,)))
    row_back = dot(plain, ret[:, half:], ((0,), (0,)))
    terms = ret.reshape(near, far, pad, width)[:, :, pad - 1, :pad].astype(F32)
    term_at = jnp.sum(jnp.where(hit, terms[:, :, :, None], 0.0), axis=(1, 2))
    term_k = jnp.sum(jnp.where(picked, term_at[None], 0.0), axis=1) / row_gate.astype(F32)
    term_k = jnp.pad(term_k, ((0, META - topk), (0, 0))).T
    send = jnp.concatenate([row_out.astype(BF), row_back.astype(BF), term_k.astype(BF)], axis=1)
    send = send.reshape(n_group, far * per_group, width + META)
    got = lax.all_to_all(send, "group", split_axis=0, concat_axis=0, tiled=True)

    got = got.reshape(groups, 2, far * per_group, width + META)
    sums = [
        dot(chooser, got[:, c].reshape(groups * far * per_group, width + META), ((0,), (0,))) for c in range(2)
    ]
    full = jnp.concatenate(
        [sums[0][:, :half], sums[1][:, :half], sums[0][:, half:width], sums[1][:, half:width], sums[0][:, width:] + sums[1][:, width:]],
        axis=1,
    ).reshape(far, tok, 2 * width + META)
    total = full[0]
    for f in range(1, far):
        total = total + shift(full[f].astype(BF), -near * f).astype(F32)
    return (
        total[:, :width].astype(BF),
        total[:, width : 2 * width].astype(BF),
        total[:, 2 * width : 2 * width + topk],
    )


def solution(mesh):
    rows = P(("group", "local"), None)
    weights = P("group", "local", None, None)
    return jax.shard_map(
        body,
        mesh=mesh,
        in_specs=(rows, rows, rows, rows, rows, weights, weights, weights),
        out_specs=(rows, rows, rows),
        check_vma=False,
    )
```

```python
import jax
import jax.numpy as jnp
from jax import lax
from jax.sharding import PartitionSpec as P

BF = jnp.bfloat16
F32 = jnp.float32
META = 128


def dot(a, b, dims):
    return lax.dot_general(a, b, (dims, ((), ())), preferred_element_type=F32)


def body(tokens, grad_mixed, gates, group_ids, expert_ids, w_gate, w_up, w_down):
    n_group = lax.axis_size("group")
    n_local = lax.axis_size("local")
    near = 8 if n_local % 8 == 0 and n_local > 8 else n_local // 2
    far = n_local // near
    groups = n_group // 2
    tok = tokens.shape[0]
    width = tokens.shape[1]
    half = width // 2
    topk = expert_ids.shape[1]
    named = group_ids.shape[1]
    per_group = named * tok // groups
    capacity = (25 * tok + n_local - 1) // n_local
    pad = (capacity // 8 + 1) * 8
    me = lax.axis_index("group")
    my_group = (me // 2).astype(BF)
    core = me % 2
    z = lax.axis_index("local")

    def shift(array, by):
        return lax.ppermute(array, "local", [(i, (i + by) % n_local) for i in range(n_local)])

    def hop(array, step, sign):
        if step == 0:
            return array
        if step != near // 2:
            return shift(array, sign * step)
        pairs = [
            (g * n_local + i, g * n_local + (i + sign * (step if g % 2 == 0 else -step)) % n_local)
            for g in range(n_group)
            for i in range(n_local)
        ]
        return lax.ppermute(array, ("group", "local"), pairs)

    def swap(array):
        return lax.ppermute(array, "group", [(i, i ^ 1) for i in range(n_group)])

    group_iota = jnp.arange(groups, dtype=jnp.int32)[None, :]
    member = jnp.zeros((tok, groups), F32)
    for n in range(named):
        member = jnp.maximum(member, (group_ids[:, n : n + 1] == group_iota).astype(F32))
    order = jnp.arange(tok, dtype=jnp.int32)
    placed = dot((order[None, :] < order[:, None]).astype(BF), member.astype(BF), ((1,), (0,)))
    code = jnp.where(member > 0, placed, -1.0)
    meta = jnp.concatenate(
        [(expert_ids // n_local).astype(BF), (expert_ids % n_local).astype(BF), gates, code.astype(BF)], axis=1
    )
    meta = jnp.pad(meta, ((0, 0), (0, META - meta.shape[1])))
    own = jnp.concatenate([tokens, grad_mixed, meta], axis=1)
    rows = lax.all_gather(
        own, "local", axis=0, tiled=True, axis_index_groups=[[b + near * f for f in range(far)] for b in range(near)]
    )

    codes = rows[:, 2 * width + 3 * topk : 2 * width + 3 * topk + groups].T
    codes = codes.astype(F32)[:, None, None, :] == jnp.arange(per_group, dtype=F32)[None, None, :, None]
    row_plane = jnp.arange(far * tok, dtype=jnp.int32) // tok
    planes = jnp.arange(far, dtype=jnp.int32)
    chooser = (codes & (row_plane[None, :] == planes[:, None])[None, :, None, :]).astype(BF)
    chooser = chooser.reshape(groups * far * per_group, far * tok)
    parts = []
    for c in range(2):
        piece = jnp.concatenate(
            [rows[:, c * half : (c + 1) * half], rows[:, width + c * half : width + (c + 1) * half], rows[:, 2 * width :]],
            axis=1,
        )
        parts.append(dot(chooser, piece, ((1,), (0,))).astype(BF).reshape(groups, 1, far * per_group, width + META))
    send = jnp.concatenate(parts, axis=1).reshape(n_group, far * per_group, width + META)
    got = lax.all_to_all(send, "group", split_axis=0, concat_axis=0, tiled=True)
    n_rows = n_group * far * per_group
    got = got.reshape(n_rows, width + META)

    steps = [near // 2] + [s for d in range(near // 2 - 1, 0, -1) for s in (d, -d)] + [0]
    info = got[:, width:].T
    row_group, row_pos, row_gate = info[:topk], info[topk : 2 * topk], info[2 * topk : 3 * topk]
    turned = jnp.where(core == 0, near // 2, n_local - near // 2)
    target = jnp.array([s % n_local for s in steps], jnp.int32).at[0].set(turned)
    target = ((z + target) % n_local).astype(BF)
    picked = (row_group == my_group)[:, None, :] & (row_pos[:, None, :] == target[None, :, None])
    counted = jnp.any(picked, axis=0)
    gate_at = jnp.sum(jnp.where(picked, row_gate.astype(F32)[:, None, :], 0.0), axis=0)
    index = jnp.arange(n_rows, dtype=jnp.int32)
    plane_of = (index // per_group) % far
    ahead = ((index[:, None] < index[None, :]) & (plane_of[:, None] == plane_of[None, :])).astype(BF)
    ranked = dot(counted.astype(BF), ahead, ((1,), (0,))).astype(jnp.int32)
    kept = counted & (ranked < capacity)
    slot = jnp.where(kept, ranked, -1)
    hit = (slot[:, None, None, :] == jnp.arange(pad, dtype=jnp.int32)[None, None, :, None]) & (
        plane_of[None, None, None, :] == jnp.arange(far, dtype=jnp.int32)[None, :, None, None]
    )
    n_slots = near * far * pad
    plain = hit.astype(BF).reshape(n_slots, n_rows)
    scaled = jnp.where(hit, gate_at[:, None, None, :], 0.0).astype(BF).reshape(n_slots, n_rows)
    slot_x = dot(plain, got[:, :half], ((1,), (0,))).astype(BF)
    slot_dy = dot(scaled, got[:, half:width], ((1,), (0,))).astype(BF)
    slots = jnp.concatenate([slot_x, slot_dy], axis=1).reshape(near, far * pad, width)
    mine = jnp.concatenate(
        [hop(slots[i], s, 1) for i, s in enumerate(steps)], axis=0
    )

    def own_first(array, axis):
        low = lax.slice_in_dim(array, 0, half, axis=axis)
        high = lax.slice_in_dim(array, half, width, axis=axis)
        return jnp.where(core == 0, low, high), jnp.where(core == 0, high, low)

    in_own, in_other = own_first(w_gate[0, 0], 0)
    lin_own, lin_other = own_first(w_up[0, 0], 0)
    out_own, out_other = own_first(w_down[0, 0], 1)
    other = swap(mine)
    pre_gate = dot(mine[:, :half], in_own, ((1,), (0,))) + dot(other[:, :half], in_other, ((1,), (0,)))
    pre_up = dot(mine[:, :half], lin_own, ((1,), (0,))) + dot(other[:, :half], lin_other, ((1,), (0,)))
    sigmoid = jax.nn.sigmoid(pre_gate)
    active = pre_gate * sigmoid
    hidden = (active * pre_up).astype(BF)
    grad_hidden = dot(mine[:, half:], out_own, ((1,), (1,))) + dot(other[:, half:], out_other, ((1,), (1,)))
    grad_pre = (grad_hidden * pre_up * sigmoid * (1.0 + pre_gate * (1.0 - sigmoid))).astype(BF)
    grad_lin = (grad_hidden * active).astype(BF)

    give_out = dot(hidden, out_other, ((1,), (0,))).astype(BF)
    give_back = (dot(grad_pre, in_other, ((1,), (1,))) + dot(grad_lin, lin_other, ((1,), (1,)))).astype(BF)
    gave = swap(jnp.concatenate([give_out, give_back], axis=1))
    sum_out = dot(hidden, out_own, ((1,), (0,))) + gave[:, :half].astype(F32)
    sum_back = (
        dot(grad_pre, in_own, ((1,), (1,))) + dot(grad_lin, lin_own, ((1,), (1,))) + gave[:, half:].astype(F32)
    )
    term = jnp.sum(mine[:, half:].astype(F32) * sum_out, axis=1, keepdims=True)
    spots = (jnp.arange(META, dtype=jnp.int32)[None, :] == jnp.arange(n_slots, dtype=jnp.int32)[:, None] % pad)
    spare = jnp.sum(jnp.where(spots, term, 0.0).reshape(near * far, pad, META), axis=1, keepdims=True)
    spare = jnp.where((jnp.arange(pad) == pad - 1)[None, :, None], spare, sum_out[:, :META].reshape(near * far, pad, META))
    ret = jnp.concatenate(
        [spare.reshape(n_slots, META).astype(BF), sum_out[:, META:].astype(BF), sum_back.astype(BF)], axis=1
    ).reshape(near, far * pad, width)
    ret = jnp.concatenate(
        [hop(ret[i], s, -1) for i, s in enumerate(steps)], axis=0
    )

    row_out = dot(scaled, ret[:, :half], ((0,), (0,)))
    row_back = dot(plain, ret[:, half:], ((0,), (0,)))
    terms = ret.reshape(near, far, pad, width)[:, :, pad - 1, :pad].astype(F32)
    term_at = jnp.sum(jnp.where(hit, terms[:, :, :, None], 0.0), axis=(1, 2))
    term_k = jnp.sum(jnp.where(picked, term_at[None], 0.0), axis=1) / row_gate.astype(F32)
    term_k = jnp.pad(term_k, ((0, META - topk), (0, 0))).T
    send = jnp.concatenate([row_out.astype(BF), row_back.astype(BF), term_k.astype(BF)], axis=1)
    send = send.reshape(n_group, far * per_group, width + META)
    got = lax.all_to_all(send, "group", split_axis=0, concat_axis=0, tiled=True)

    wanted = (z // near + planes) % far
    turned = chooser.reshape(groups * far * per_group, far, tok)
    turned = jnp.concatenate([jnp.take(turned, wanted[d], axis=1) for d in range(far)], axis=1)
    got = got.reshape(groups, 2, far * per_group, width + META)
    sums = [
        dot(turned, got[:, c].reshape(groups * far * per_group, width + META), ((0,), (0,))) for c in range(2)
    ]
    full = jnp.concatenate(
        [sums[0][:, :half], sums[1][:, :half], sums[0][:, half:width], sums[1][:, half:width], sums[0][:, width:] + sums[1][:, width:]],
        axis=1,
    ).reshape(far, tok, 2 * width + META)
    total = full[0]
    for f in range(1, far):
        total = total + shift(full[f].astype(BF), near * f).astype(F32)
    return (
        total[:, :width].astype(BF),
        total[:, width : 2 * width].astype(BF),
        total[:, 2 * width : 2 * width + topk],
    )


def solution(mesh):
    rows = P(("group", "local"), None)
    weights = P("group", "local", None, None)
    return jax.shard_map(
        body,
        mesh=mesh,
        in_specs=(rows, rows, rows, rows, rows, weights, weights, weights),
        out_specs=(rows, rows, rows),
        check_vma=False,
    )
```

```python
import functools

import jax
import jax.numpy as jnp
from jax import lax
from jax.experimental import pallas as pl
from jax.experimental.pallas import tpu as pltpu
from jax.sharding import PartitionSpec as P

BF = jnp.bfloat16
F32 = jnp.float32
META = 128


def dot(a, b, dims):
    return lax.dot_general(a, b, (dims, ((), ())), preferred_element_type=F32)


def whole(kernel, outs, flops, *args, scalars=0):
    vmem = pl.BlockSpec(memory_space=pltpu.VMEM)
    smem = pl.BlockSpec(memory_space=pltpu.SMEM)
    moved = sum(a.size * a.dtype.itemsize for a in args)
    return pl.pallas_call(
        kernel,
        out_shape=outs,
        in_specs=[smem] * scalars + [vmem] * (len(args) - scalars),
        out_specs=jax.tree.map(lambda _: vmem, outs),
        compiler_params=pltpu.CompilerParams(vmem_limit_bytes=24 * 1024 * 1024),
        cost_estimate=pl.CostEstimate(flops=flops, bytes_accessed=moved, transcendentals=0),
    )(*args)


def pack_kernel(n_local, groups, x_ref, dy_ref, gate_ref, group_ref, expert_ref, own_ref):
    tok, width = x_ref.shape
    topk = expert_ref.shape[1]
    member = jnp.zeros((tok, groups), F32)
    iota = lax.broadcasted_iota(jnp.int32, (tok, groups), 1)
    for n in range(group_ref.shape[1]):
        member = jnp.where(group_ref[:, n : n + 1] == iota, 1.0, member)
    lower = lax.broadcasted_iota(jnp.int32, (tok, tok), 1) < lax.broadcasted_iota(jnp.int32, (tok, tok), 0)
    placed = dot(jnp.where(lower, 1.0, 0.0).astype(BF), member.astype(BF), ((1,), (0,)))
    code = jnp.where(member > 0, placed, -1.0)
    ids = expert_ref[...]
    shift = n_local.bit_length() - 1
    pieces = (
        lax.shift_right_logical(ids, shift).astype(F32).astype(BF),
        (ids & (n_local - 1)).astype(F32).astype(BF),
        gate_ref[...],
        code.astype(BF),
    )
    meta = jnp.zeros((tok, META), F32)
    start = 0
    for piece in pieces:
        n = piece.shape[1]
        spot = lax.broadcasted_iota(jnp.int32, (n, META), 1) == lax.broadcasted_iota(jnp.int32, (n, META), 0) + start
        meta = meta + dot(piece, jnp.where(spot, 1.0, 0.0).astype(BF), ((1,), (0,)))
        start += n
    own_ref[:, :width] = x_ref[...]
    own_ref[:, width : 2 * width] = dy_ref[...]
    own_ref[:, 2 * width :] = meta.astype(BF)


def halves_of(core_ref, half):
    own = pl.multiple_of(core_ref[0] * half, half)
    other = pl.multiple_of((1 - core_ref[0]) * half, half)
    return pl.ds(own, half), pl.ds(other, half)


def expert_kernel(core_ref, mine, other, w_in, w_lin, w_out, hidden_ref, pre_ref, lin_ref, give_ref):
    half = mine.shape[1] // 2
    own, far = halves_of(core_ref, half)
    mine_x, other_x = mine[:, :half], other[:, :half]
    pre_gate = dot(mine_x, w_in[own, :], ((1,), (0,))) + dot(other_x, w_in[far, :], ((1,), (0,)))
    pre_up = dot(mine_x, w_lin[own, :], ((1,), (0,))) + dot(other_x, w_lin[far, :], ((1,), (0,)))
    sigmoid = jax.nn.sigmoid(pre_gate)
    active = pre_gate * sigmoid
    hidden = (active * pre_up).astype(BF)
    hidden_ref[...] = hidden
    grad_hidden = dot(mine[:, half:], w_out[:, own], ((1,), (1,))) + dot(other[:, half:], w_out[:, far], ((1,), (1,)))
    grad_pre = (grad_hidden * pre_up * sigmoid * (1.0 + pre_gate * (1.0 - sigmoid))).astype(BF)
    grad_lin = (grad_hidden * active).astype(BF)
    pre_ref[...] = grad_pre
    lin_ref[...] = grad_lin
    give_ref[:, :half] = dot(hidden, w_out[:, far], ((1,), (0,))).astype(BF)
    back = dot(grad_pre, w_in[far, :], ((1,), (1,))) + dot(grad_lin, w_lin[far, :], ((1,), (1,)))
    give_ref[:, half:] = back.astype(BF)


def keep_kernel(core_ref, hidden, grad_pre, grad_lin, w_in, w_lin, w_out, keep_ref):
    half = w_in.shape[0] // 2
    own, _ = halves_of(core_ref, half)
    keep_ref[:, :half] = dot(hidden[...], w_out[:, own], ((1,), (0,)))
    back = dot(grad_pre[...], w_in[own, :], ((1,), (1,))) + dot(grad_lin[...], w_lin[own, :], ((1,), (1,)))
    keep_ref[:, half:] = back


def merge_kernel(pad, keep, gave, mine, ret_ref):
    n_slots, width = mine.shape
    half = width // 2
    sum_out = keep[:, :half] + gave[:, :half].astype(F32)
    term = jnp.sum(mine[:, half:].astype(F32) * sum_out, axis=1, keepdims=True)
    row = lax.broadcasted_iota(jnp.int32, (n_slots, META), 0) & (pad - 1)
    lane = lax.broadcasted_iota(jnp.int32, (n_slots, META), 1)
    spots = jnp.where(lane == row, jnp.broadcast_to(term, (n_slots, META)), 0.0)
    spare = jnp.sum(spots.reshape(n_slots // pad, pad, META), axis=1, keepdims=True)
    spare = jnp.broadcast_to(spare, (n_slots // pad, pad, META)).reshape(n_slots, META)
    ret_ref[:, :half] = sum_out.astype(BF)
    ret_ref[:, :META] = jnp.where(row == pad - 1, spare, sum_out[:, :META]).astype(BF)
    ret_ref[:, half:] = (keep[:, half:] + gave[:, half:].astype(F32)).astype(BF)


def body(tokens, grad_mixed, gates, group_ids, expert_ids, w_gate, w_up, w_down):
    n_group = lax.axis_size("group")
    n_local = lax.axis_size("local")
    near = 8 if n_local % 8 == 0 and n_local > 8 else n_local // 2
    far = n_local // near
    groups = n_group // 2
    tok = tokens.shape[0]
    width = tokens.shape[1]
    half = width // 2
    topk = expert_ids.shape[1]
    named = group_ids.shape[1]
    per_group = named * tok // groups
    capacity = (25 * tok + n_local - 1) // n_local
    pad = (capacity // 8 + 1) * 8
    me = lax.axis_index("group")
    my_group = (me // 2).astype(BF)
    core = me % 2
    z = lax.axis_index("local")

    def shift(array, by):
        return lax.ppermute(array, "local", [(i, (i + by) % n_local) for i in range(n_local)])

    def hop(array, step, sign):
        if step == 0:
            return array
        if step != near // 2:
            return shift(array, sign * step)
        pairs = [
            (g * n_local + i, g * n_local + (i + sign * (step if g % 2 == 0 else -step)) % n_local)
            for g in range(n_group)
            for i in range(n_local)
        ]
        return lax.ppermute(array, ("group", "local"), pairs)

    def swap(array):
        return lax.ppermute(array, "group", [(i, i ^ 1) for i in range(n_group)])

    own = whole(
        functools.partial(pack_kernel, n_local, groups),
        jax.ShapeDtypeStruct((tok, 2 * width + META), BF),
        4 * tok * META * topk,
        tokens,
        grad_mixed,
        gates,
        group_ids,
        expert_ids,
    )
    rows = lax.all_gather(
        own, "local", axis=0, tiled=True, axis_index_groups=[[b + near * f for f in range(far)] for b in range(near)]
    )

    codes = rows[:, 2 * width + 3 * topk : 2 * width + 3 * topk + groups].T
    codes = codes.astype(F32)[:, None, None, :] == jnp.arange(per_group, dtype=F32)[None, None, :, None]
    row_plane = jnp.arange(far * tok, dtype=jnp.int32) // tok
    planes = jnp.arange(far, dtype=jnp.int32)
    chooser = (codes & (row_plane[None, :] == planes[:, None])[None, :, None, :]).astype(BF)
    chooser = chooser.reshape(groups * far * per_group, far * tok)
    parts = []
    for c in range(2):
        piece = jnp.concatenate(
            [rows[:, c * half : (c + 1) * half], rows[:, width + c * half : width + (c + 1) * half], rows[:, 2 * width :]],
            axis=1,
        )
        parts.append(dot(chooser, piece, ((1,), (0,))).astype(BF).reshape(groups, 1, far * per_group, width + META))
    send = jnp.concatenate(parts, axis=1).reshape(n_group, far * per_group, width + META)
    got = lax.all_to_all(send, "group", split_axis=0, concat_axis=0, tiled=True)
    n_rows = n_group * far * per_group
    got = got.reshape(n_rows, width + META)

    steps = [near // 2] + [s for d in range(near // 2 - 1, 0, -1) for s in (d, -d)] + [0]
    info = got[:, width:].T
    row_group, row_pos, row_gate = info[:topk], info[topk : 2 * topk], info[2 * topk : 3 * topk]
    turned = jnp.where(core == 0, near // 2, n_local - near // 2)
    target = jnp.array([s % n_local for s in steps], jnp.int32).at[0].set(turned)
    target = ((z + target) % n_local).astype(BF)
    picked = (row_group == my_group)[:, None, :] & (row_pos[:, None, :] == target[None, :, None])
    counted = jnp.any(picked, axis=0)
    gate_at = jnp.sum(jnp.where(picked, row_gate.astype(F32)[:, None, :], 0.0), axis=0)
    index = jnp.arange(n_rows, dtype=jnp.int32)
    plane_of = (index // per_group) % far
    ahead = ((index[:, None] < index[None, :]) & (plane_of[:, None] == plane_of[None, :])).astype(BF)
    ranked = dot(counted.astype(BF), ahead, ((1,), (0,))).astype(jnp.int32)
    kept = counted & (ranked < capacity)
    slot = jnp.where(kept, ranked, -1)
    hit = (slot[:, None, None, :] == jnp.arange(pad, dtype=jnp.int32)[None, None, :, None]) & (
        plane_of[None, None, None, :] == jnp.arange(far, dtype=jnp.int32)[None, :, None, None]
    )
    n_slots = near * far * pad
    plain = hit.astype(BF).reshape(n_slots, n_rows)
    scaled = jnp.where(hit, gate_at[:, None, None, :], 0.0).astype(BF).reshape(n_slots, n_rows)
    slot_x = dot(plain, got[:, :half], ((1,), (0,))).astype(BF)
    slot_dy = dot(scaled, got[:, half:width], ((1,), (0,))).astype(BF)
    slots = jnp.concatenate([slot_x, slot_dy], axis=1).reshape(near, far * pad, width)
    mine = jnp.concatenate(
        [hop(slots[i], s, 1) for i, s in enumerate(steps)], axis=0
    )

    other = swap(mine)
    which = core.reshape(1)
    weights = (w_gate[0, 0], w_up[0, 0], w_down[0, 0])
    hid = w_up.shape[3]
    narrow = jax.ShapeDtypeStruct((n_slots, hid), BF)
    wide = jax.ShapeDtypeStruct((n_slots, width), BF)
    products = 2 * n_slots * width * hid
    hidden, grad_pre, grad_lin, give = whole(
        expert_kernel, (narrow, narrow, narrow, wide), 9 * products // 2, which, mine, other, *weights, scalars=1
    )

    gave = swap(give)
    keep = whole(
        keep_kernel,
        jax.ShapeDtypeStruct((n_slots, width), F32),
        3 * products // 2,
        which,
        hidden,
        grad_pre,
        grad_lin,
        *weights,
        scalars=1,
    )
    ret = whole(functools.partial(merge_kernel, pad), wide, 4 * n_slots * width, keep, gave, mine)
    ret = ret.reshape(near, far * pad, width)
    ret = jnp.concatenate(
        [hop(ret[i], s, -1) for i, s in enumerate(steps)], axis=0
    )

    row_out = dot(scaled, ret[:, :half], ((0,), (0,)))
    row_back = dot(plain, ret[:, half:], ((0,), (0,)))
    terms = ret.reshape(near, far, pad, width)[:, :, pad - 1, :pad].astype(F32)
    term_at = jnp.sum(jnp.where(hit, terms[:, :, :, None], 0.0), axis=(1, 2))
    term_k = jnp.sum(jnp.where(picked, term_at[None], 0.0), axis=1) / row_gate.astype(F32)
    term_k = jnp.pad(term_k, ((0, META - topk), (0, 0))).T
    send = jnp.concatenate([row_out.astype(BF), row_back.astype(BF), term_k.astype(BF)], axis=1)
    send = send.reshape(n_group, far * per_group, width + META)
    got = lax.all_to_all(send, "group", split_axis=0, concat_axis=0, tiled=True)

    wanted = (z // near + planes) % far
    turned = chooser.reshape(groups * far * per_group, far, tok)
    turned = jnp.concatenate([jnp.take(turned, wanted[d], axis=1) for d in range(far)], axis=1)
    got = got.reshape(groups, 2, far * per_group, width + META)
    sums = [
        dot(turned, got[:, c].reshape(groups * far * per_group, width + META), ((0,), (0,))) for c in range(2)
    ]
    full = jnp.concatenate(
        [sums[0][:, :half], sums[1][:, :half], sums[0][:, half:width], sums[1][:, half:width], sums[0][:, width:] + sums[1][:, width:]],
        axis=1,
    ).reshape(far, tok, 2 * width + META)
    total = full[0]
    if far == 4:
        up = shift(full[2][:, :width].astype(BF), near).astype(F32)
        down = shift(full[2][:, width:].astype(BF), -near).astype(F32)
        above = jnp.concatenate([full[1][:, :width] + up, full[1][:, width:]], axis=1)
        below = jnp.concatenate([full[3][:, :width], full[3][:, width:] + down], axis=1)
        total = total + shift(above.astype(BF), near).astype(F32) + shift(below.astype(BF), -near).astype(F32)
    else:
        for f in range(1, far):
            total = total + shift(full[f].astype(BF), near * f).astype(F32)
    return (
        total[:, :width].astype(BF),
        total[:, width : 2 * width].astype(BF),
        total[:, 2 * width : 2 * width + topk],
    )


def solution(mesh):
    rows = P(("group", "local"), None)
    weights = P("group", "local", None, None)
    return jax.shard_map(
        body,
        mesh=mesh,
        in_specs=(rows, rows, rows, rows, rows, weights, weights, weights),
        out_specs=(rows, rows, rows),
        check_vma=False,
    )
```

```python
import functools

import jax
import jax.numpy as jnp
from jax import lax
from jax.experimental import pallas as pl
from jax.experimental.pallas import tpu as pltpu
from jax.sharding import PartitionSpec as P

BF = jnp.bfloat16
F32 = jnp.float32
META = 128


def dot(a, b, dims):
    return lax.dot_general(a, b, (dims, ((), ())), preferred_element_type=F32)


def whole(kernel, outs, flops, *args, scalars=0):
    vmem = pl.BlockSpec(memory_space=pltpu.VMEM)
    smem = pl.BlockSpec(memory_space=pltpu.SMEM)
    moved = sum(a.size * a.dtype.itemsize for a in args)
    return pl.pallas_call(
        kernel,
        out_shape=outs,
        in_specs=[smem] * scalars + [vmem] * (len(args) - scalars),
        out_specs=jax.tree.map(lambda _: vmem, outs),
        compiler_params=pltpu.CompilerParams(vmem_limit_bytes=24 * 1024 * 1024),
        cost_estimate=pl.CostEstimate(flops=flops, bytes_accessed=moved, transcendentals=0),
    )(*args)


def pack_kernel(n_local, groups, x_ref, dy_ref, gate_ref, group_ref, expert_ref, own_ref):
    tok, width = x_ref.shape
    topk = expert_ref.shape[1]
    member = jnp.zeros((tok, groups), F32)
    iota = lax.broadcasted_iota(jnp.int32, (tok, groups), 1)
    for n in range(group_ref.shape[1]):
        member = jnp.where(group_ref[:, n : n + 1] == iota, 1.0, member)
    lower = lax.broadcasted_iota(jnp.int32, (tok, tok), 1) < lax.broadcasted_iota(jnp.int32, (tok, tok), 0)
    placed = dot(jnp.where(lower, 1.0, 0.0).astype(BF), member.astype(BF), ((1,), (0,)))
    code = jnp.where(member > 0, placed, -1.0)
    ids = expert_ref[...]
    shift = n_local.bit_length() - 1
    pieces = (
        lax.shift_right_logical(ids, shift).astype(F32).astype(BF),
        (ids & (n_local - 1)).astype(F32).astype(BF),
        gate_ref[...],
        code.astype(BF),
    )
    meta = jnp.zeros((tok, META), F32)
    start = 0
    for piece in pieces:
        n = piece.shape[1]
        spot = lax.broadcasted_iota(jnp.int32, (n, META), 1) == lax.broadcasted_iota(jnp.int32, (n, META), 0) + start
        meta = meta + dot(piece, jnp.where(spot, 1.0, 0.0).astype(BF), ((1,), (0,)))
        start += n
    own_ref[:, :width] = x_ref[...]
    own_ref[:, width : 2 * width] = dy_ref[...]
    own_ref[:, 2 * width :] = meta.astype(BF)


def halves_of(core_ref, half):
    own = pl.multiple_of(core_ref[0] * half, half)
    other = pl.multiple_of((1 - core_ref[0]) * half, half)
    return pl.ds(own, half), pl.ds(other, half)


def expert_kernel(core_ref, mine, other, w_in, w_lin, w_out, hidden_ref, pre_ref, lin_ref, give_ref):
    half = mine.shape[1] // 2
    own, far = halves_of(core_ref, half)
    mine_x, other_x = mine[:, :half], other[:, :half]
    pre_gate = dot(mine_x, w_in[own, :], ((1,), (0,))) + dot(other_x, w_in[far, :], ((1,), (0,)))
    pre_up = dot(mine_x, w_lin[own, :], ((1,), (0,))) + dot(other_x, w_lin[far, :], ((1,), (0,)))
    sigmoid = jax.nn.sigmoid(pre_gate)
    active = pre_gate * sigmoid
    hidden = (active * pre_up).astype(BF)
    hidden_ref[...] = hidden
    grad_hidden = dot(mine[:, half:], w_out[:, own], ((1,), (1,))) + dot(other[:, half:], w_out[:, far], ((1,), (1,)))
    grad_pre = (grad_hidden * pre_up * sigmoid * (1.0 + pre_gate * (1.0 - sigmoid))).astype(BF)
    grad_lin = (grad_hidden * active).astype(BF)
    pre_ref[...] = grad_pre
    lin_ref[...] = grad_lin
    give_ref[:, :half] = dot(hidden, w_out[:, far], ((1,), (0,))).astype(BF)
    back = dot(grad_pre, w_in[far, :], ((1,), (1,))) + dot(grad_lin, w_lin[far, :], ((1,), (1,)))
    give_ref[:, half:] = back.astype(BF)


def keep_kernel(core_ref, hidden, grad_pre, grad_lin, w_in, w_lin, w_out, keep_ref):
    half = w_in.shape[0] // 2
    own, _ = halves_of(core_ref, half)
    keep_ref[:, :half] = dot(hidden[...], w_out[:, own], ((1,), (0,)))
    back = dot(grad_pre[...], w_in[own, :], ((1,), (1,))) + dot(grad_lin[...], w_lin[own, :], ((1,), (1,)))
    keep_ref[:, half:] = back


def merge_kernel(pad, keep, gave, mine, *ret_refs):
    n_slots, width = mine.shape
    half = width // 2
    sum_out = keep[:, :half] + gave[:, :half].astype(F32)
    term = jnp.sum(mine[:, half:].astype(F32) * sum_out, axis=1, keepdims=True)
    row = lax.broadcasted_iota(jnp.int32, (n_slots, META), 0) & (pad - 1)
    lane = lax.broadcasted_iota(jnp.int32, (n_slots, META), 1)
    spots = jnp.where(lane == row, jnp.broadcast_to(term, (n_slots, META)), 0.0)
    spare = jnp.sum(spots.reshape(n_slots // pad, pad, META), axis=1, keepdims=True)
    spare = jnp.broadcast_to(spare, (n_slots // pad, pad, META)).reshape(n_slots, META)
    first = jnp.where(row == pad - 1, spare, sum_out[:, :META])
    back = keep[:, half:] + gave[:, half:].astype(F32)
    rows = n_slots // len(ret_refs)
    for i, ref in enumerate(ret_refs):
        at = slice(i * rows, (i + 1) * rows)
        ref[:, :META] = first[at].astype(BF)
        ref[:, META:half] = sum_out[at, META:].astype(BF)
        ref[:, half:] = back[at].astype(BF)


def body(tokens, grad_mixed, gates, group_ids, expert_ids, w_gate, w_up, w_down):
    n_group = lax.axis_size("group")
    n_local = lax.axis_size("local")
    near = 8 if n_local % 8 == 0 and n_local > 8 else n_local // 2
    far = n_local // near
    groups = n_group // 2
    tok = tokens.shape[0]
    width = tokens.shape[1]
    half = width // 2
    topk = expert_ids.shape[1]
    named = group_ids.shape[1]
    per_group = named * tok // groups
    capacity = (25 * tok + n_local - 1) // n_local
    pad = (capacity // 8 + 1) * 8
    me = lax.axis_index("group")
    my_group = (me // 2).astype(BF)
    core = me % 2
    z = lax.axis_index("local")

    def shift(array, by):
        return lax.ppermute(array, "local", [(i, (i + by) % n_local) for i in range(n_local)])

    def hop(array, step, sign):
        if step == 0:
            return array
        if step != near // 2:
            return shift(array, sign * step)
        pairs = [
            (g * n_local + i, g * n_local + (i + sign * (step if g % 2 == 0 else -step)) % n_local)
            for g in range(n_group)
            for i in range(n_local)
        ]
        return lax.ppermute(array, ("group", "local"), pairs)

    def swap(array):
        return lax.ppermute(array, "group", [(i, i ^ 1) for i in range(n_group)])

    own = whole(
        functools.partial(pack_kernel, n_local, groups),
        jax.ShapeDtypeStruct((tok, 2 * width + META), BF),
        4 * tok * META * topk,
        tokens,
        grad_mixed,
        gates,
        group_ids,
        expert_ids,
    )
    rows = lax.all_gather(
        own, "local", axis=0, tiled=True, axis_index_groups=[[b + near * f for f in range(far)] for b in range(near)]
    )

    codes = rows[:, 2 * width + 3 * topk : 2 * width + 3 * topk + groups].T
    codes = codes.astype(F32)[:, None, None, :] == jnp.arange(per_group, dtype=F32)[None, None, :, None]
    row_plane = jnp.arange(far * tok, dtype=jnp.int32) // tok
    planes = jnp.arange(far, dtype=jnp.int32)
    chooser = (codes & (row_plane[None, :] == planes[:, None])[None, :, None, :]).astype(BF)
    chooser = chooser.reshape(groups * far * per_group, far * tok)
    parts = []
    for c in range(2):
        piece = jnp.concatenate(
            [rows[:, c * half : (c + 1) * half], rows[:, width + c * half : width + (c + 1) * half], rows[:, 2 * width :]],
            axis=1,
        )
        parts.append(dot(chooser, piece, ((1,), (0,))).astype(BF).reshape(groups, 1, far * per_group, width + META))
    send = jnp.concatenate(parts, axis=1).reshape(n_group, far * per_group, width + META)
    got = lax.all_to_all(send, "group", split_axis=0, concat_axis=0, tiled=True)
    n_rows = n_group * far * per_group
    got = got.reshape(n_rows, width + META)

    steps = [near // 2] + [s for d in range(near // 2 - 1, 0, -1) for s in (d, -d)] + [0]
    info = got[:, width:].T
    row_group, row_pos, row_gate = info[:topk], info[topk : 2 * topk], info[2 * topk : 3 * topk]
    turned = jnp.where(core == 0, near // 2, n_local - near // 2)
    target = jnp.array([s % n_local for s in steps], jnp.int32).at[0].set(turned)
    target = ((z + target) % n_local).astype(BF)
    picked = (row_group == my_group)[:, None, :] & (row_pos[:, None, :] == target[None, :, None])
    counted = jnp.any(picked, axis=0)
    gate_at = jnp.sum(jnp.where(picked, row_gate.astype(F32)[:, None, :], 0.0), axis=0)
    index = jnp.arange(n_rows, dtype=jnp.int32)
    plane_of = (index // per_group) % far
    ahead = ((index[:, None] < index[None, :]) & (plane_of[:, None] == plane_of[None, :])).astype(BF)
    ranked = dot(counted.astype(BF), ahead, ((1,), (0,))).astype(jnp.int32)
    kept = counted & (ranked < capacity)
    slot = jnp.where(kept, ranked, -1)
    hit = (slot[:, None, None, :] == jnp.arange(pad, dtype=jnp.int32)[None, None, :, None]) & (
        plane_of[None, None, None, :] == jnp.arange(far, dtype=jnp.int32)[None, :, None, None]
    )
    n_slots = near * far * pad
    plain = hit.astype(BF).reshape(n_slots, n_rows)
    scaled = jnp.where(hit, gate_at[:, None, None, :], 0.0).astype(BF).reshape(n_slots, n_rows)
    slot_x = dot(plain, got[:, :half], ((1,), (0,))).astype(BF)
    slot_dy = dot(scaled, got[:, half:width], ((1,), (0,))).astype(BF)
    slots = jnp.concatenate([slot_x, slot_dy], axis=1).reshape(near, far * pad, width)
    mine = jnp.concatenate(
        [hop(slots[i], s, 1) for i, s in enumerate(steps)], axis=0
    )

    other = swap(mine)
    which = core.reshape(1)
    weights = (w_gate[0, 0], w_up[0, 0], w_down[0, 0])
    hid = w_up.shape[3]
    narrow = jax.ShapeDtypeStruct((n_slots, hid), BF)
    wide = jax.ShapeDtypeStruct((n_slots, width), BF)
    products = 2 * n_slots * width * hid
    hidden, grad_pre, grad_lin, give = whole(
        expert_kernel, (narrow, narrow, narrow, wide), 9 * products // 2, which, mine, other, *weights, scalars=1
    )

    gave = swap(give)
    keep = whole(
        keep_kernel,
        jax.ShapeDtypeStruct((n_slots, width), F32),
        3 * products // 2,
        which,
        hidden,
        grad_pre,
        grad_lin,
        *weights,
        scalars=1,
    )
    block = jax.ShapeDtypeStruct((far * pad, width), BF)
    ret = whole(functools.partial(merge_kernel, pad), (block,) * near, 4 * n_slots * width, keep, gave, mine)
    ret = jnp.concatenate(
        [hop(ret[i], s, -1) for i, s in enumerate(steps)], axis=0
    )

    row_out = dot(scaled, ret[:, :half], ((0,), (0,)))
    row_back = dot(plain, ret[:, half:], ((0,), (0,)))
    terms = ret.reshape(near, far, pad, width)[:, :, pad - 1, :pad].astype(F32)
    term_at = jnp.sum(jnp.where(hit, terms[:, :, :, None], 0.0), axis=(1, 2))
    term_k = jnp.sum(jnp.where(picked, term_at[None], 0.0), axis=1) / row_gate.astype(F32)
    term_k = jnp.pad(term_k, ((0, META - topk), (0, 0))).T
    send = jnp.concatenate([row_out.astype(BF), row_back.astype(BF), term_k.astype(BF)], axis=1)
    send = send.reshape(n_group, far * per_group, width + META)
    got = lax.all_to_all(send, "group", split_axis=0, concat_axis=0, tiled=True)

    wanted = (z // near + planes) % far
    turned = chooser.reshape(groups * far * per_group, far, tok)
    turned = jnp.concatenate([jnp.take(turned, wanted[d], axis=1) for d in range(far)], axis=1)
    got = got.reshape(groups, 2, far * per_group, width + META)
    sums = [
        dot(turned, got[:, c].reshape(groups * far * per_group, width + META), ((0,), (0,))) for c in range(2)
    ]
    full = jnp.concatenate(
        [sums[0][:, :half], sums[1][:, :half], sums[0][:, half:width], sums[1][:, half:width], sums[0][:, width:] + sums[1][:, width:]],
        axis=1,
    ).reshape(far, tok, 2 * width + META)
    total = full[0]
    for f in sorted(range(1, far), key=lambda f: -min(f, far - f)):
        total = total + shift(full[f].astype(BF), near * f).astype(F32)
    return (
        total[:, :width].astype(BF),
        total[:, width : 2 * width].astype(BF),
        total[:, 2 * width : 2 * width + topk],
    )


def solution(mesh):
    rows = P(("group", "local"), None)
    weights = P("group", "local", None, None)
    return jax.shard_map(
        body,
        mesh=mesh,
        in_specs=(rows, rows, rows, rows, rows, weights, weights, weights),
        out_specs=(rows, rows, rows),
        check_vma=False,
    )
```

```python
import functools

import jax
import jax.numpy as jnp
from jax import lax
from jax.experimental import pallas as pl
from jax.experimental.pallas import tpu as pltpu
from jax.sharding import PartitionSpec as P

BF = jnp.bfloat16
F32 = jnp.float32
META = 128


def dot(a, b, dims):
    return lax.dot_general(a, b, (dims, ((), ())), preferred_element_type=F32)


def whole(kernel, outs, flops, *args, scalars=0):
    vmem = pl.BlockSpec(memory_space=pltpu.VMEM)
    smem = pl.BlockSpec(memory_space=pltpu.SMEM)
    moved = sum(a.size * a.dtype.itemsize for a in args)
    return pl.pallas_call(
        kernel,
        out_shape=outs,
        in_specs=[smem] * scalars + [vmem] * (len(args) - scalars),
        out_specs=jax.tree.map(lambda _: vmem, outs),
        compiler_params=pltpu.CompilerParams(vmem_limit_bytes=24 * 1024 * 1024),
        cost_estimate=pl.CostEstimate(flops=flops, bytes_accessed=moved, transcendentals=0),
    )(*args)


def pack_kernel(n_local, groups, *refs):
    own_ref, sems = refs[5], refs[11]
    copies = [pltpu.make_async_copy(refs[i], refs[6 + i], sems.at[i]) for i in range(5)]
    for copy in copies:
        copy.start()
    for copy in copies:
        copy.wait()
    x_ref, dy_ref, gate_ref, group_ref, expert_ref = refs[6:11]
    tok, width = x_ref.shape
    member = jnp.zeros((groups, tok), F32)
    iota = lax.broadcasted_iota(jnp.int32, (groups, tok), 0)
    for n in range(group_ref.shape[0]):
        member = jnp.where(group_ref[n : n + 1, :] == iota, 1.0, member)
    upper = lax.broadcasted_iota(jnp.int32, (tok, tok), 0) < lax.broadcasted_iota(jnp.int32, (tok, tok), 1)
    placed = dot(member.astype(BF), jnp.where(upper, 1.0, 0.0).astype(BF), ((1,), (0,)))
    code = jnp.where(member > 0, placed, -1.0)
    ids = expert_ref[...]
    shift = n_local.bit_length() - 1
    pieces = (
        lax.shift_right_logical(ids, shift).astype(F32).astype(BF),
        (ids & (n_local - 1)).astype(F32).astype(BF),
        gate_ref[...],
        code.T.astype(BF),
    )
    meta = jnp.zeros((tok, META), F32)
    start = 0
    for piece in pieces:
        n = piece.shape[1]
        spot = lax.broadcasted_iota(jnp.int32, (n, META), 1) == lax.broadcasted_iota(jnp.int32, (n, META), 0) + start
        meta = meta + dot(piece, jnp.where(spot, 1.0, 0.0).astype(BF), ((1,), (0,)))
        start += n
    own_ref[:, :width] = x_ref[...]
    own_ref[:, width : 2 * width] = dy_ref[...]
    own_ref[:, 2 * width :] = meta.astype(BF)


def halves_of(core_ref, half):
    own = pl.multiple_of(core_ref[0] * half, half)
    other = pl.multiple_of((1 - core_ref[0]) * half, half)
    return pl.ds(own, half), pl.ds(other, half)


def expert_kernel(core_ref, mine, other, w_in, w_lin, w_out, hidden_ref, pre_ref, lin_ref, give_ref):
    half = mine.shape[1] // 2
    own, far = halves_of(core_ref, half)
    mine_x, other_x = mine[:, :half], other[:, :half]
    pre_gate = dot(mine_x, w_in[own, :], ((1,), (0,))) + dot(other_x, w_in[far, :], ((1,), (0,)))
    pre_up = dot(mine_x, w_lin[own, :], ((1,), (0,))) + dot(other_x, w_lin[far, :], ((1,), (0,)))
    sigmoid = jax.nn.sigmoid(pre_gate)
    active = pre_gate * sigmoid
    hidden = (active * pre_up).astype(BF)
    hidden_ref[...] = hidden
    grad_hidden = dot(mine[:, half:], w_out[:, own], ((1,), (1,))) + dot(other[:, half:], w_out[:, far], ((1,), (1,)))
    grad_pre = (grad_hidden * pre_up * sigmoid * (1.0 + pre_gate * (1.0 - sigmoid))).astype(BF)
    grad_lin = (grad_hidden * active).astype(BF)
    pre_ref[...] = grad_pre
    lin_ref[...] = grad_lin
    give_ref[:, :half] = dot(hidden, w_out[:, far], ((1,), (0,))).astype(BF)
    back = dot(grad_pre, w_in[far, :], ((1,), (1,))) + dot(grad_lin, w_lin[far, :], ((1,), (1,)))
    give_ref[:, half:] = back.astype(BF)


def keep_kernel(core_ref, hidden, grad_pre, grad_lin, w_in, w_lin, w_out, keep_ref):
    half = w_in.shape[0] // 2
    own, _ = halves_of(core_ref, half)
    keep_ref[:, :half] = dot(hidden[...], w_out[:, own], ((1,), (0,)))
    back = dot(grad_pre[...], w_in[own, :], ((1,), (1,))) + dot(grad_lin[...], w_lin[own, :], ((1,), (1,)))
    keep_ref[:, half:] = back


def merge_kernel(pad, keep, gave, mine, *ret_refs):
    n_slots, width = mine.shape
    half = width // 2
    sum_out = keep[:, :half] + gave[:, :half].astype(F32)
    term = jnp.sum(mine[:, half:].astype(F32) * sum_out, axis=1, keepdims=True)
    row = lax.broadcasted_iota(jnp.int32, (n_slots, META), 0) & (pad - 1)
    lane = lax.broadcasted_iota(jnp.int32, (n_slots, META), 1)
    spots = jnp.where(lane == row, jnp.broadcast_to(term, (n_slots, META)), 0.0)
    spare = jnp.sum(spots.reshape(n_slots // pad, pad, META), axis=1, keepdims=True)
    spare = jnp.broadcast_to(spare, (n_slots // pad, pad, META)).reshape(n_slots, META)
    first = jnp.where(row == pad - 1, spare, sum_out[:, :META])
    back = keep[:, half:] + gave[:, half:].astype(F32)
    rows = n_slots // len(ret_refs)
    for i, ref in enumerate(ret_refs):
        at = slice(i * rows, (i + 1) * rows)
        ref[:, :META] = first[at].astype(BF)
        ref[:, META:half] = sum_out[at, META:].astype(BF)
        ref[:, half:] = back[at].astype(BF)


def body(tokens, grad_mixed, gates, group_ids, expert_ids, w_gate, w_up, w_down):
    n_group = lax.axis_size("group")
    n_local = lax.axis_size("local")
    near = 8 if n_local % 8 == 0 and n_local > 8 else n_local // 2
    far = n_local // near
    groups = n_group // 2
    tok = tokens.shape[0]
    width = tokens.shape[1]
    half = width // 2
    topk = expert_ids.shape[1]
    named = group_ids.shape[1]
    per_group = named * tok // groups
    capacity = (25 * tok + n_local - 1) // n_local
    pad = (capacity // 8 + 1) * 8
    me = lax.axis_index("group")
    my_group = (me // 2).astype(BF)
    core = me % 2
    z = lax.axis_index("local")

    def shift(array, by):
        return lax.ppermute(array, "local", [(i, (i + by) % n_local) for i in range(n_local)])

    def hop(array, step, sign):
        if step == 0:
            return array
        if step != near // 2:
            return shift(array, sign * step)
        pairs = [
            (g * n_local + i, g * n_local + (i + sign * (step if g % 2 == 0 else -step)) % n_local)
            for g in range(n_group)
            for i in range(n_local)
        ]
        return lax.ppermute(array, ("group", "local"), pairs)

    def swap(array):
        return lax.ppermute(array, "group", [(i, i ^ 1) for i in range(n_group)])

    parts = (tokens, grad_mixed, gates, group_ids.T, expert_ids)
    own = pl.pallas_call(
        functools.partial(pack_kernel, n_local, groups),
        out_shape=jax.ShapeDtypeStruct((tok, 2 * width + META), BF),
        in_specs=[pl.BlockSpec(memory_space=pl.ANY)] * 5,
        out_specs=pl.BlockSpec(memory_space=pltpu.VMEM),
        scratch_shapes=[pltpu.VMEM(p.shape, p.dtype) for p in parts] + [pltpu.SemaphoreType.DMA((5,))],
        cost_estimate=pl.CostEstimate(flops=tok * META * 100, bytes_accessed=8 * tok * width, transcendentals=0),
    )(*parts)
    rows = lax.all_gather(
        own, "local", axis=0, tiled=True, axis_index_groups=[[b + near * f for f in range(far)] for b in range(near)]
    )

    codes = rows[:, 2 * width + 3 * topk : 2 * width + 3 * topk + groups].T
    codes = codes.astype(F32)[:, None, None, :] == jnp.arange(per_group, dtype=F32)[None, None, :, None]
    row_plane = jnp.arange(far * tok, dtype=jnp.int32) // tok
    away = sorted(range(far), key=lambda f: -min(f, far - f))
    planes = (z // near + jnp.array(away, jnp.int32)) % far
    chooser = (codes & (row_plane[None, :] == planes[:, None])[None, :, None, :]).astype(BF)
    chooser = chooser.reshape(groups * far * per_group, far * tok)
    parts = []
    for c in range(2):
        piece = jnp.concatenate(
            [rows[:, c * half : (c + 1) * half], rows[:, width + c * half : width + (c + 1) * half], rows[:, 2 * width :]],
            axis=1,
        )
        parts.append(dot(chooser, piece, ((1,), (0,))).astype(BF).reshape(groups, 1, far * per_group, width + META))
    send = jnp.concatenate(parts, axis=1).reshape(n_group, far * per_group, width + META)
    got = lax.all_to_all(send, "group", split_axis=0, concat_axis=0, tiled=True)
    n_rows = n_group * far * per_group
    got = got.reshape(n_rows, width + META)

    steps = [near // 2] + [s for d in range(near // 2 - 1, 0, -1) for s in (d, -d)] + [0]
    info = got[:, width:].T
    row_group, row_pos, row_gate = info[:topk], info[topk : 2 * topk], info[2 * topk : 3 * topk]
    turned = jnp.where(core == 0, near // 2, n_local - near // 2)
    target = jnp.array([s % n_local for s in steps], jnp.int32).at[0].set(turned)
    target = ((z + target) % n_local).astype(BF)
    picked = (row_group == my_group)[:, None, :] & (row_pos[:, None, :] == target[None, :, None])
    counted = jnp.any(picked, axis=0)
    gate_at = jnp.sum(jnp.where(picked, row_gate.astype(F32)[:, None, :], 0.0), axis=0)
    index = jnp.arange(n_rows, dtype=jnp.int32)
    plane_of = (index // per_group) % far
    ahead = ((index[:, None] < index[None, :]) & (plane_of[:, None] == plane_of[None, :])).astype(BF)
    ranked = dot(counted.astype(BF), ahead, ((1,), (0,))).astype(jnp.int32)
    kept = counted & (ranked < capacity)
    slot = jnp.where(kept, ranked, -1)
    plane_at = (z // near + sum(jnp.where(plane_of == q, f, 0) for q, f in enumerate(away))) % far
    hit = (slot[:, None, None, :] == jnp.arange(pad, dtype=jnp.int32)[None, None, :, None]) & (
        plane_at[None, None, None, :] == jnp.arange(far, dtype=jnp.int32)[None, :, None, None]
    )
    n_slots = near * far * pad
    plain = hit.astype(BF).reshape(n_slots, n_rows)
    scaled = jnp.where(hit, gate_at[:, None, None, :], 0.0).astype(BF).reshape(n_slots, n_rows)
    slot_x = dot(plain, got[:, :half], ((1,), (0,))).astype(BF)
    slot_dy = dot(scaled, got[:, half:width], ((1,), (0,))).astype(BF)
    slots = jnp.concatenate([slot_x, slot_dy], axis=1).reshape(near, far * pad, width)
    mine = jnp.concatenate(
        [hop(slots[i], s, 1) for i, s in enumerate(steps)], axis=0
    )

    other = swap(mine)
    which = core.reshape(1)
    weights = (w_gate[0, 0], w_up[0, 0], w_down[0, 0])
    hid = w_up.shape[3]
    narrow = jax.ShapeDtypeStruct((n_slots, hid), BF)
    wide = jax.ShapeDtypeStruct((n_slots, width), BF)
    products = 2 * n_slots * width * hid
    hidden, grad_pre, grad_lin, give = whole(
        expert_kernel, (narrow, narrow, narrow, wide), 9 * products // 2, which, mine, other, *weights, scalars=1
    )

    gave = swap(give)
    keep = whole(
        keep_kernel,
        jax.ShapeDtypeStruct((n_slots, width), F32),
        3 * products // 2,
        which,
        hidden,
        grad_pre,
        grad_lin,
        *weights,
        scalars=1,
    )
    block = jax.ShapeDtypeStruct((far * pad, width), BF)
    ret = whole(functools.partial(merge_kernel, pad), (block,) * near, 4 * n_slots * width, keep, gave, mine)
    ret = jnp.concatenate(
        [hop(ret[i], s, -1) for i, s in enumerate(steps)], axis=0
    )

    row_out = dot(scaled, ret[:, :half], ((0,), (0,)))
    row_back = dot(plain, ret[:, half:], ((0,), (0,)))
    terms = ret.reshape(near, far, pad, width)[:, :, pad - 1, :pad].astype(F32)
    term_at = jnp.sum(jnp.where(hit, terms[:, :, :, None], 0.0), axis=(1, 2))
    term_k = jnp.sum(jnp.where(picked, term_at[None], 0.0), axis=1) / row_gate.astype(F32)
    term_k = jnp.pad(term_k, ((0, META - topk), (0, 0))).T
    send = jnp.concatenate([row_out.astype(BF), row_back.astype(BF), term_k.astype(BF)], axis=1)
    send = send.reshape(n_group, far * per_group, width + META)

    lone = jnp.sum(chooser.reshape(groups, far, per_group, far, tok), axis=3)

    def to_tokens(low, high):
        got = lax.all_to_all(
            send[:, low * per_group : high * per_group], "group", split_axis=0, concat_axis=0, tiled=True
        )
        count = high - low
        picks = lone[:, low:high, :, None, :] * jnp.eye(count, dtype=BF)[None, :, None, :, None]
        picks = picks.reshape(groups * count * per_group, count * tok)
        got = got.reshape(groups, 2, count * per_group, width + META)
        sums = [dot(picks, got[:, c].reshape(groups * count * per_group, width + META), ((0,), (0,))) for c in range(2)]
        return jnp.concatenate(
            [
                sums[0][:, :half],
                sums[1][:, :half],
                sums[0][:, half:width],
                sums[1][:, half:width],
                sums[0][:, width:] + sums[1][:, width:],
            ],
            axis=1,
        )

    first = shift(to_tokens(0, 1).astype(BF), near * away[0])
    full = to_tokens(1, far).reshape(far - 1, tok, 2 * width + META)
    total = full[far - 2]
    for q in range(1, far - 1):
        total = total + shift(full[q - 1].astype(BF), near * away[q]).astype(F32)
    total = total + first.astype(F32)
    return (
        total[:, :width].astype(BF),
        total[:, width : 2 * width].astype(BF),
        total[:, 2 * width : 2 * width + topk],
    )


def solution(mesh):
    rows = P(("group", "local"), None)
    weights = P("group", "local", None, None)
    return jax.shard_map(
        body,
        mesh=mesh,
        in_specs=(rows, rows, rows, rows, rows, weights, weights, weights),
        out_specs=(rows, rows, rows),
        check_vma=False,
    )
```

```python
import functools

import jax
import jax.numpy as jnp
from jax import lax
from jax.experimental import pallas as pl
from jax.experimental.pallas import tpu as pltpu
from jax.sharding import PartitionSpec as P

BF = jnp.bfloat16
F32 = jnp.float32
META = 128


def dot(a, b, dims):
    return lax.dot_general(a, b, (dims, ((), ())), preferred_element_type=F32)


def whole(kernel, outs, flops, *args, scalars=0):
    vmem = pl.BlockSpec(memory_space=pltpu.VMEM)
    smem = pl.BlockSpec(memory_space=pltpu.SMEM)
    moved = sum(a.size * a.dtype.itemsize for a in args)
    return pl.pallas_call(
        kernel,
        out_shape=outs,
        in_specs=[smem] * scalars + [vmem] * (len(args) - scalars),
        out_specs=jax.tree.map(lambda _: vmem, outs),
        compiler_params=pltpu.CompilerParams(vmem_limit_bytes=24 * 1024 * 1024),
        cost_estimate=pl.CostEstimate(flops=flops, bytes_accessed=moved, transcendentals=0),
    )(*args)


def pack_kernel(n_local, groups, *refs):
    own_ref, sems = refs[5], refs[11]
    copies = [pltpu.make_async_copy(refs[i], refs[6 + i], sems.at[i]) for i in range(5)]
    for copy in copies:
        copy.start()
    for copy in copies:
        copy.wait()
    x_ref, dy_ref, gate_ref, group_ref, expert_ref = refs[6:11]
    tok, width = x_ref.shape
    member = jnp.zeros((groups, tok), F32)
    iota = lax.broadcasted_iota(jnp.int32, (groups, tok), 0)
    for n in range(group_ref.shape[0]):
        member = jnp.where(group_ref[n : n + 1, :] == iota, 1.0, member)
    upper = lax.broadcasted_iota(jnp.int32, (tok, tok), 0) < lax.broadcasted_iota(jnp.int32, (tok, tok), 1)
    placed = dot(member.astype(BF), jnp.where(upper, 1.0, 0.0).astype(BF), ((1,), (0,)))
    code = jnp.where(member > 0, placed, -1.0)
    ids = expert_ref[...]
    shift = n_local.bit_length() - 1
    pieces = (
        lax.shift_right_logical(ids, shift).astype(F32).astype(BF),
        (ids & (n_local - 1)).astype(F32).astype(BF),
        gate_ref[...],
        code.T.astype(BF),
    )
    meta = jnp.zeros((tok, META), F32)
    start = 0
    for piece in pieces:
        n = piece.shape[1]
        spot = lax.broadcasted_iota(jnp.int32, (n, META), 1) == lax.broadcasted_iota(jnp.int32, (n, META), 0) + start
        meta = meta + dot(piece, jnp.where(spot, 1.0, 0.0).astype(BF), ((1,), (0,)))
        start += n
    own_ref[:, :width] = x_ref[...]
    own_ref[:, width : 2 * width] = dy_ref[...]
    own_ref[:, 2 * width :] = meta.astype(BF)


def halves_of(core_ref, half):
    own = pl.multiple_of(core_ref[0] * half, half)
    other = pl.multiple_of((1 - core_ref[0]) * half, half)
    return pl.ds(own, half), pl.ds(other, half)


def expert_kernel(core_ref, mine, other, w_in, w_lin, w_out, hidden_ref, pre_ref, lin_ref, give_ref):
    half = mine.shape[1] // 2
    own, far = halves_of(core_ref, half)
    mine_x, other_x = mine[:, :half], other[:, :half]
    pre_gate = dot(mine_x, w_in[own, :], ((1,), (0,))) + dot(other_x, w_in[far, :], ((1,), (0,)))
    pre_up = dot(mine_x, w_lin[own, :], ((1,), (0,))) + dot(other_x, w_lin[far, :], ((1,), (0,)))
    sigmoid = jax.nn.sigmoid(pre_gate)
    active = pre_gate * sigmoid
    hidden = (active * pre_up).astype(BF)
    hidden_ref[...] = hidden
    grad_hidden = dot(mine[:, half:], w_out[:, own], ((1,), (1,))) + dot(other[:, half:], w_out[:, far], ((1,), (1,)))
    grad_pre = (grad_hidden * pre_up * sigmoid * (1.0 + pre_gate * (1.0 - sigmoid))).astype(BF)
    grad_lin = (grad_hidden * active).astype(BF)
    pre_ref[...] = grad_pre
    lin_ref[...] = grad_lin
    give_ref[:, :half] = dot(hidden, w_out[:, far], ((1,), (0,))).astype(BF)
    back = dot(grad_pre, w_in[far, :], ((1,), (1,))) + dot(grad_lin, w_lin[far, :], ((1,), (1,)))
    give_ref[:, half:] = back.astype(BF)


def keep_kernel(core_ref, hidden, grad_pre, grad_lin, w_in, w_lin, w_out, keep_ref):
    half = w_in.shape[0] // 2
    own, _ = halves_of(core_ref, half)
    keep_ref[:, :half] = dot(hidden[...], w_out[:, own], ((1,), (0,)))
    back = dot(grad_pre[...], w_in[own, :], ((1,), (1,))) + dot(grad_lin[...], w_lin[own, :], ((1,), (1,)))
    keep_ref[:, half:] = back


def merge_kernel(pad, keep, gave, mine, *ret_refs):
    n_slots, width = mine.shape
    half = width // 2
    sum_out = keep[:, :half] + gave[:, :half].astype(F32)
    term = jnp.sum(mine[:, half:].astype(F32) * sum_out, axis=1, keepdims=True)
    row = lax.broadcasted_iota(jnp.int32, (n_slots, META), 0) & (pad - 1)
    lane = lax.broadcasted_iota(jnp.int32, (n_slots, META), 1)
    spots = jnp.where(lane == row, jnp.broadcast_to(term, (n_slots, META)), 0.0)
    spare = jnp.sum(spots.reshape(n_slots // pad, pad, META), axis=1, keepdims=True)
    spare = jnp.broadcast_to(spare, (n_slots // pad, pad, META)).reshape(n_slots, META)
    first = jnp.where(row == pad - 1, spare, sum_out[:, :META])
    back = keep[:, half:] + gave[:, half:].astype(F32)
    rows = n_slots // len(ret_refs)
    for i, ref in enumerate(ret_refs):
        at = slice(i * rows, (i + 1) * rows)
        ref[:, :META] = first[at].astype(BF)
        ref[:, META:half] = sum_out[at, META:].astype(BF)
        ref[:, half:] = back[at].astype(BF)


def body(tokens, grad_mixed, gates, group_ids, expert_ids, w_gate, w_up, w_down):
    n_group = lax.axis_size("group")
    n_local = lax.axis_size("local")
    near = 8 if n_local % 8 == 0 and n_local > 8 else n_local // 2
    far = n_local // near
    groups = n_group // 2
    tok = tokens.shape[0]
    width = tokens.shape[1]
    half = width // 2
    topk = expert_ids.shape[1]
    named = group_ids.shape[1]
    per_group = named * tok // groups
    capacity = (25 * tok + n_local - 1) // n_local
    pad = (capacity // 8 + 1) * 8
    me = lax.axis_index("group")
    my_group = (me // 2).astype(BF)
    core = me % 2
    z = lax.axis_index("local")

    def shift(array, by):
        return lax.ppermute(array, "local", [(i, (i + by) % n_local) for i in range(n_local)])

    def split(array, step):
        pairs = [
            (g * n_local + i, g * n_local + (i + (step if g % 2 == 0 else -step)) % n_local)
            for g in range(n_group)
            for i in range(n_local)
        ]
        return lax.ppermute(array, ("group", "local"), pairs)

    def hop(array, step, sign):
        if step == 0:
            return array
        return split(array, sign * step) if step == near // 2 else shift(array, sign * step)

    def swap(array):
        return lax.ppermute(array, "group", [(i, i ^ 1) for i in range(n_group)])

    parts = (tokens, grad_mixed, gates, group_ids.T, expert_ids)
    own = pl.pallas_call(
        functools.partial(pack_kernel, n_local, groups),
        out_shape=jax.ShapeDtypeStruct((tok, 2 * width + META), BF),
        in_specs=[pl.BlockSpec(memory_space=pl.ANY)] * 5,
        out_specs=pl.BlockSpec(memory_space=pltpu.VMEM),
        scratch_shapes=[pltpu.VMEM(p.shape, p.dtype) for p in parts] + [pltpu.SemaphoreType.DMA((5,))],
        cost_estimate=pl.CostEstimate(flops=tok * META * 100, bytes_accessed=8 * tok * width, transcendentals=0),
    )(*parts)
    rows = lax.all_gather(
        own, "local", axis=0, tiled=True, axis_index_groups=[[b + near * f for f in range(far)] for b in range(near)]
    )

    def codes_of(info):
        codes = info[:, 3 * topk : 3 * topk + groups].T.astype(F32)
        return codes[:, None, None, :] == jnp.arange(per_group, dtype=F32)[None, None, :, None]

    info = rows[:, 2 * width :]
    partner = swap(info)
    row_plane = jnp.arange(far * tok, dtype=jnp.int32) // tok
    away = sorted(range(far), key=lambda f: -min(f, far - f))
    planes = (z // near + jnp.array(away, jnp.int32)) % far
    def chooser_of(info):
        return (codes_of(info) & (row_plane[None, :] == planes[:, None])[None, :, None, :]).astype(BF)

    chooser = chooser_of(info).reshape(groups * far * per_group, far * tok)
    parts = []
    for c in range(2):
        piece = jnp.concatenate(
            [rows[:, c * half : (c + 1) * half], rows[:, width + c * half : width + (c + 1) * half], rows[:, 2 * width :]],
            axis=1,
        )
        parts.append(dot(chooser, piece, ((1,), (0,))).astype(BF).reshape(groups, 1, far * per_group, width + META))
    send = jnp.concatenate(parts, axis=1).reshape(n_group, far * per_group, width + META)
    got = lax.all_to_all(send, "group", split_axis=0, concat_axis=0, tiled=True)
    n_rows = n_group * far * per_group
    got = got.reshape(n_rows, width + META)

    steps = [near // 2] + [s for d in range(near // 2 - 1, 0, -1) for s in (d, -d)] + [0]
    facts = got[:, width:].T
    row_group, row_pos, row_gate = facts[:topk], facts[topk : 2 * topk], facts[2 * topk : 3 * topk]
    turned = jnp.where(core == 0, near // 2, n_local - near // 2)
    target = jnp.array([s % n_local for s in steps], jnp.int32).at[0].set(turned)
    target = ((z + target) % n_local).astype(BF)
    picked = (row_group == my_group)[:, None, :] & (row_pos[:, None, :] == target[None, :, None])
    counted = jnp.any(picked, axis=0)
    gate_at = jnp.sum(jnp.where(picked, row_gate.astype(F32)[:, None, :], 0.0), axis=0)
    index = jnp.arange(n_rows, dtype=jnp.int32)
    plane_of = (index // per_group) % far
    ahead = ((index[:, None] < index[None, :]) & (plane_of[:, None] == plane_of[None, :])).astype(BF)
    ranked = dot(counted.astype(BF), ahead, ((1,), (0,))).astype(jnp.int32)
    kept = counted & (ranked < capacity)
    slot = jnp.where(kept, ranked, -1)
    plane_at = (z // near + sum(jnp.where(plane_of == q, f, 0) for q, f in enumerate(away))) % far
    hit = (slot[:, None, None, :] == jnp.arange(pad, dtype=jnp.int32)[None, None, :, None]) & (
        plane_at[None, None, None, :] == jnp.arange(far, dtype=jnp.int32)[None, :, None, None]
    )
    n_slots = near * far * pad
    plain = hit.astype(BF).reshape(n_slots, n_rows)
    scaled = jnp.where(hit, gate_at[:, None, None, :], 0.0).astype(BF).reshape(n_slots, n_rows)
    slot_x = dot(plain, got[:, :half], ((1,), (0,))).astype(BF)
    slot_dy = dot(scaled, got[:, half:width], ((1,), (0,))).astype(BF)
    slots = jnp.concatenate([slot_x, slot_dy], axis=1).reshape(near, far * pad, width)
    mine = jnp.concatenate(
        [hop(slots[i], s, 1) for i, s in enumerate(steps)], axis=0
    )

    other = swap(mine)
    which = core.reshape(1)
    weights = (w_gate[0, 0], w_up[0, 0], w_down[0, 0])
    hid = w_up.shape[3]
    narrow = jax.ShapeDtypeStruct((n_slots, hid), BF)
    wide = jax.ShapeDtypeStruct((n_slots, width), BF)
    products = 2 * n_slots * width * hid
    hidden, grad_pre, grad_lin, give = whole(
        expert_kernel, (narrow, narrow, narrow, wide), 9 * products // 2, which, mine, other, *weights, scalars=1
    )

    gave = swap(give)
    keep = whole(
        keep_kernel,
        jax.ShapeDtypeStruct((n_slots, width), F32),
        3 * products // 2,
        which,
        hidden,
        grad_pre,
        grad_lin,
        *weights,
        scalars=1,
    )
    block = jax.ShapeDtypeStruct((far * pad, width), BF)
    ret = whole(functools.partial(merge_kernel, pad), (block,) * near, 4 * n_slots * width, keep, gave, mine)
    ret = jnp.concatenate(
        [hop(ret[i], s, -1) for i, s in enumerate(steps)], axis=0
    )

    row_out = dot(scaled, ret[:, :half], ((0,), (0,)))
    row_back = dot(plain, ret[:, half:], ((0,), (0,)))
    terms = ret.reshape(near, far, pad, width)[:, :, pad - 1, :pad].astype(F32)
    term_at = jnp.sum(jnp.where(hit, terms[:, :, :, None], 0.0), axis=(1, 2))
    term_k = jnp.sum(jnp.where(picked, term_at[None], 0.0), axis=1) / row_gate.astype(F32)
    term_k = jnp.pad(term_k, ((0, META - topk), (0, 0))).T
    send = jnp.concatenate([row_out.astype(BF), row_back.astype(BF), term_k.astype(BF)], axis=1)

    source = jnp.arange(n_rows, dtype=jnp.int32).reshape(groups, 2, far, per_group)

    def moved(order):
        order = order.reshape(-1)
        return dot((order[:, None] == jnp.arange(n_rows, dtype=jnp.int32)[None, :]).astype(BF), send, ((1,), (0,))).astype(BF)

    def lone_of(info):
        return jnp.sum(chooser_of(info).reshape(groups, far, per_group, far, tok), axis=3)

    def diagonal(picks):
        picks = picks[:, :, :, None, :] * jnp.eye(2, dtype=BF)[None, :, None, :, None]
        return picks.reshape(groups, 2 * per_group, 2 * tok)

    def gathered(array, picks):
        count, lanes = picks.shape[1], array.shape[-1]
        array = array.reshape(n_group, count, lanes)
        array = lax.all_to_all(array, "group", split_axis=0, concat_axis=0, tiled=True)
        array = array.reshape(groups, 2, count, lanes)
        picks = picks.reshape(groups * count, -1)
        return [dot(picks, array[:, c].reshape(groups * count, lanes), ((0,), (0,))) for c in range(2)]

    mine_lone, partner_lone = lone_of(info), lone_of(partner)
    both = jnp.stack(
        [jnp.where(core == 0, mine_lone, partner_lone), jnp.where(core == 0, partner_lone, mine_lone)], axis=1
    )
    order = jnp.stack([source[:, :, 0], source[:, :, 0]], axis=1).reshape(-1)
    outs = moved(order)
    upward = (jnp.arange(order.shape[0], dtype=jnp.int32) // (2 * per_group) % 2 == 0)[:, None]
    outs = jnp.concatenate([jnp.where(upward, outs[:, :half], outs[:, half:width]), outs[:, width:]], axis=1)
    sums = gathered(outs, diagonal(both[:, :, 0]))
    relay = jnp.concatenate([sums[0][:, :half], sums[1][:, :half], sums[0][:, half:] + sums[1][:, half:]], axis=1)
    relay = split(relay.astype(BF), near).astype(F32)

    sides = jnp.stack([source[:, :, 1], source[:, :, 2]], axis=1).reshape(groups, 2, 2 * per_group)
    blank = jnp.full((groups, 2, per_group), n_rows, jnp.int32)
    sides = jnp.concatenate([source[:, :, far - 1], sides, blank], axis=2)
    beside = diagonal(jnp.where(core == 0, both[:, :, 1], both[:, :, 2]))
    picks = jnp.concatenate(
        [
            jnp.pad(mine_lone[:, far - 1], ((0, 0), (0, 0), (0, 2 * tok))),
            jnp.pad(beside, ((0, 0), (0, per_group), (tok, 0))),
        ],
        axis=1,
    )
    sums = gathered(moved(sides), picks)
    full = jnp.concatenate(
        [
            sums[0][:, :half],
            sums[1][:, :half],
            sums[0][:, half:width],
            sums[1][:, half:width],
            sums[0][:, width:] + sums[1][:, width:],
        ],
        axis=1,
    )
    even = core == 0
    pair = full[tok:] + jnp.concatenate(
        [
            jnp.where(even, relay[:, :width], 0.0),
            jnp.where(even, 0.0, relay[:, :width]),
            jnp.where(even, 0.0, relay[:, width:]),
        ],
        axis=1,
    )
    pair = split(pair.astype(BF), near)
    theirs = swap(jnp.where(even, pair[tok:], pair[:tok]))
    ours = jnp.where(even, pair[:tok], pair[tok:])
    total = full[:tok] + ours.astype(F32) + theirs.astype(F32)
    return (
        total[:, :width].astype(BF),
        total[:, width : 2 * width].astype(BF),
        total[:, 2 * width : 2 * width + topk],
    )


def solution(mesh):
    rows = P(("group", "local"), None)
    weights = P("group", "local", None, None)
    return jax.shard_map(
        body,
        mesh=mesh,
        in_specs=(rows, rows, rows, rows, rows, weights, weights, weights),
        out_specs=(rows, rows, rows),
        check_vma=False,
    )
```
